32 devices in a mesh: tm: 4 (over y, x), rows: 4 (over z), cols: 2 (over core).
Axes of the slice: x: 2, y: 2, z: 4, core: 2. Of those that a mesh axis runs over, the one named last changes fastest.
Arguments:
- latent_video: bfloat16 [24, 128, 64, 128], P('tm', 'rows', 'cols'), may hold values from -6 to 6
- input_kernel: bfloat16 [3, 3, 128, 256], replicated, may hold values from -0.1875 to 0.1875
- output_kernel: bfloat16 [3, 3, 256, 128], replicated, may hold values from -0.125 to 0.125
- decay_rate: float32 [24, 256], P('tm'), may hold values from 0.4 to 0.999, as said below
- skip_gain: float32 [128], replicated, may hold values from 0.25 to 1.75
Outputs:
- layer_output: bfloat16 [24, 128, 64, 128], P('tm', 'rows', 'cols')
The draws below stay inside these ranges and needn't reach their ends.
Inputs may be any that keep to these rules, and one draw needn't show every extreme that they name: `decay_rate`: every decay factor lies strictly between zero and one.
All inputs are finite; a program needn't handle non-finite values.
Results may differ from the reference program's by a relative error of at most 0.0048.
Values may be sent and summed in bfloat16 or wider, within the bound.
A program may use at most 128 MiB of HBM per device.

```python
import jax
import jax.numpy as jnp
from jax import lax

CIN = 128
STATE = 256
TOTAL_FRAMES = 24
HEIGHT = 128
WIDTH = 64


def draw_decay_rate(key, part):
    random_seeds = jax.random.split(jax.random.fold_in(key, 17), 6)
    fast = jax.random.bernoulli(random_seeds[0], 0.5, (STATE,))
    slow_loss = jax.random.uniform(random_seeds[1], (STATE,), jnp.float32, 0.02, 0.4)
    slow_rate = jnp.exp(-slow_loss / TOTAL_FRAMES)
    fast_span = jax.random.uniform(random_seeds[2], (STATE,), jnp.float32, 30.0, 50.0)
    fast_rate = jnp.exp(-2.302585 / fast_span)
    baseline_forget = jnp.where(fast, fast_rate, slow_rate)
    jitter_loss = jax.random.uniform(random_seeds[3], (TOTAL_FRAMES, STATE), jnp.float32, 0.0, 0.3)
    wobble_factor = jnp.exp(-jitter_loss / TOTAL_FRAMES)
    spike_frames = jax.random.randint(random_seeds[4], (2,), 0, TOTAL_FRAMES)
    frame_numbers = jnp.arange(TOTAL_FRAMES, dtype=jnp.int32)
    spike_flag = jnp.any(frame_numbers[:, None] == spike_frames[None, :], axis=1)[:, None]
    spike_scale = jax.random.uniform(random_seeds[5], (TOTAL_FRAMES, 1), jnp.float32, 0.55, 0.8)
    forget_speeds = baseline_forget[None, :] * wobble_factor * jnp.where(spike_flag, spike_scale, 1.0)
    return jnp.clip(forget_speeds, 0.25, 0.999).astype(jnp.float32)


def level_of(own_key, extent, pieces, smallest, top_value):
    factor_of, own = 1.0, jax.random.fold_in(own_key, 6)
    for axis_at, shards_of in pieces:
        steps = jnp.exp(jax.random.uniform(jax.random.fold_in(own, axis_at), (shards_of,), jnp.float32, smallest / len(pieces), top_value / len(pieces)))
        factor_of = factor_of * jnp.repeat(steps, extent[axis_at] // shards_of).reshape([-1 if axis == axis_at else 1 for axis in range(len(extent))])
    return factor_of


def centred(key, shape, deviation, bound, cuts=(), kind=jnp.bfloat16):
    gain = level_of(key, shape, cuts, -0.22, 0.18) if cuts else 1.0
    drawn = jax.random.normal(key, shape, jnp.float32) * deviation * gain
    return jnp.minimum(jnp.maximum(drawn, -bound), bound).astype(kind)


def setup_inputs(seed: int = 0) -> dict:
    key_list = jax.random.split(jax.random.key(seed), 6)
    return {
        "latent_video": centred(key_list[0], (TOTAL_FRAMES, HEIGHT, WIDTH, CIN), 1.0, 6.0, ((0, 4), (1, 4), (2, 2))),
        "input_kernel": centred(key_list[1], (3, 3, CIN, STATE), (9 * CIN) ** -0.5, 0.1875),
        "output_kernel": centred(key_list[2], (3, 3, STATE, CIN), (9 * STATE) ** -0.5, 0.125),
        "decay_rate": draw_decay_rate(jax.random.fold_in(key_list[5], 71), 0),
        "skip_gain": jnp.clip(1.0 + 0.15 * jax.random.normal(key_list[4], (CIN,), jnp.float32), 0.25, 1.75),
    }


def stencil(field, kernel):
    height = field.shape[1] - 2
    width = field.shape[2] - 2
    summed = jnp.zeros((field.shape[0], height, width, kernel.shape[3]), jnp.float32)
    for row_off in range(3):
        for col_off in range(3):
            window = field[:, row_off:row_off + height, col_off:col_off + width, :].astype(jnp.float32)
            summed = summed + jnp.einsum("fhwc,cs->fhws", window, kernel[row_off, col_off].astype(jnp.float32))
    return summed


def advance(running, inputs):
    drive_now, rate_now = inputs
    running = rate_now * running + drive_now
    return running, running


def reference(latent_video, input_kernel, output_kernel, decay_rate, skip_gain):
    padded = jnp.pad(latent_video, ((0, 0), (1, 1), (1, 1), (0, 0)))
    drive = stencil(padded, input_kernel)
    start = jnp.zeros((HEIGHT, WIDTH, STATE), jnp.float32)
    last_state, states = lax.scan(advance, start, (drive, decay_rate))
    rounded_states = states.astype(jnp.bfloat16)
    cycle = jnp.pad(rounded_states, ((0, 0), (1, 1), (1, 1), (0, 0)))
    mixed = stencil(cycle, output_kernel) + skip_gain * latent_video.astype(jnp.float32)
    return mixed.astype(jnp.bfloat16)
```

```python
import functools

import jax
import jax.numpy as jnp
from jax import lax
from jax.experimental import pallas as pl
from jax.experimental.pallas import tpu as pltpu
from jax.sharding import PartitionSpec as P

MESH = pl.DeviceIdType.MESH
STEP = 2
LAG = 3


def layer_kernel(
    blocks, tiles, x_ref, w1_ref, w2_ref, decay_ref, skip_ref, out_ref,
    xp, xs, local, st, w1, w2, decay, skip, carry_in, carry_out, result,
    load_sem, w2_sem, side_send, side_recv, z_send, z_recv,
    carry_send, carry_recv, out_sem, out_send, out_recv,
):
    frames, tile_h, tile_w, cin = x_ref.shape
    state = w1.shape[1]
    half = tile_h // 2
    width = 2 * tile_w
    chunks = (half + 2) // STEP
    flat = STEP * width
    t = lax.axis_index("tm")
    z = lax.axis_index("rows")
    c = lax.axis_index("cols")
    o = 1 - c
    has_up = z > 0
    has_down = z < tiles - 1
    has_next = t < blocks - 1
    own_cols = pl.ds(pl.multiple_of(c * tile_w, tile_w), tile_w)
    other_cols = pl.ds(pl.multiple_of(o * tile_w, tile_w), tile_w)

    loads = [
        pltpu.make_async_copy(
            x_ref.at[:, pl.ds((half - 2) * c, half + 2)],
            xp.at[:, pl.ds(2 * o, half + 2), own_cols],
            load_sem.at[0],
        ),
        pltpu.make_async_copy(w1_ref, w1, load_sem.at[1]),
        pltpu.make_async_copy(decay_ref, decay, load_sem.at[2]),
        pltpu.make_async_copy(skip_ref, skip, load_sem.at[3]),
    ]
    w2_loads = [
        pltpu.make_async_copy(
            w2_ref.at[a, b],
            w2.at[pl.ds(a * state, state), pl.ds(b * cin, cin)],
            w2_sem.at[3 * a + b],
        )
        for a in range(3)
        for b in range(3)
    ]
    for copy in loads + w2_loads:
        copy.start()

    barrier = pltpu.get_barrier_semaphore()
    up_side = jnp.logical_and(c == 0, has_up)
    down_side = jnp.logical_and(c == 1, has_down)
    pl.semaphore_signal(barrier, inc=1, device_id=(t, z, o), device_id_type=MESH)

    @pl.when(up_side)
    def _():
        for core in range(2):
            pl.semaphore_signal(barrier, inc=1, device_id=(t, z - 1, core), device_id_type=MESH)

    @pl.when(down_side)
    def _():
        for core in range(2):
            pl.semaphore_signal(barrier, inc=1, device_id=(t, z + 1, core), device_id_type=MESH)

    @pl.when(t > 0)
    def _():
        pl.semaphore_signal(barrier, inc=1, device_id=(t - 1, z, c), device_id_type=MESH)

    @pl.when(jnp.logical_and(c == 0, z == 0))
    def _():
        xp[:, 0:2] = jnp.zeros((frames, 2, width, cin), xp.dtype)

    @pl.when(jnp.logical_and(c == 1, z == tiles - 1))
    def _():
        xp[:, half + 2 : half + 4] = jnp.zeros((frames, 2, width, cin), xp.dtype)

    @pl.when(t == 0)
    def _():
        carry_in[...] = jnp.zeros_like(carry_in)

    expected = (
        1 + has_up.astype(jnp.int32) + has_down.astype(jnp.int32) + has_next.astype(jnp.int32)
    )
    pl.semaphore_wait(barrier, expected)

    side = pltpu.make_async_remote_copy(
        src_ref=x_ref.at[:, pl.ds((half - 2) * o, half + 2)],
        dst_ref=xp.at[:, pl.ds(2 * c, half + 2), own_cols],
        send_sem=side_send,
        recv_sem=side_recv,
        device_id=(t, z, o),
        device_id_type=MESH,
    )
    side.start()

    def to_down():
        return pltpu.make_async_remote_copy(
            src_ref=x_ref.at[:, pl.ds(tile_h - 2, 2)],
            dst_ref=xp.at[:, pl.ds(0, 2), own_cols],
            send_sem=z_send.at[0],
            recv_sem=z_recv.at[c],
            device_id=(t, z + 1, 0),
            device_id_type=MESH,
        )

    def to_up():
        return pltpu.make_async_remote_copy(
            src_ref=x_ref.at[:, pl.ds(0, 2)],
            dst_ref=xp.at[:, pl.ds(half + 2, 2), own_cols],
            send_sem=z_send.at[1],
            recv_sem=z_recv.at[c],
            device_id=(t, z - 1, 1),
            device_id_type=MESH,
        )

    @pl.when(has_down)
    def _():
        to_down().start()

    @pl.when(has_up)
    def _():
        to_up().start()

    for copy in loads:
        copy.wait()
    pltpu.make_async_remote_copy(
        src_ref=x_ref.at[:, pl.ds((half - 2) * o, half + 2)],
        dst_ref=xp.at[:, pl.ds(2 * o, half + 2), other_cols],
        send_sem=side_send,
        recv_sem=side_recv,
        device_id=(t, z, o),
        device_id_type=MESH,
    ).wait_recv()

    def columns(rows):
        return lax.rem(lax.broadcasted_iota(jnp.int32, (rows, 128), 0), width)

    def spread(row):
        view = xp[:, pl.ds(row, STEP)].reshape(frames * flat, cin)
        wide = view.astype(jnp.float32)
        at = columns(frames * flat)
        left = jnp.where(at == 0, 0.0, pltpu.roll(wide, 1, 0))
        right = jnp.where(at == width - 1, 0.0, pltpu.roll(wide, frames * flat - 1, 0))
        shape = (frames, STEP, width, cin)
        xs[:, pl.ds(row, STEP), :, 0:cin] = left.astype(xs.dtype).reshape(shape)
        xs[:, pl.ds(row, STEP), :, cin : 2 * cin] = view.reshape(shape)
        xs[:, pl.ds(row, STEP), :, 2 * cin : 3 * cin] = right.astype(xs.dtype).reshape(shape)

    def drive_chunk(k):
        @pl.when(k == 0)
        def _():
            spread((half + 2) * o)

        @pl.when(k == chunks - 1)
        def _():
            @pl.when(jnp.logical_or(up_side, down_side))
            def _():
                for core in range(2):
                    rows = pl.ds((half + 2) * c, 2)
                    pltpu.make_async_remote_copy(
                        src_ref=x_ref.at[:, pl.ds(0, 2)],
                        dst_ref=xp.at[:, rows, pl.ds(core * tile_w, tile_w)],
                        send_sem=z_send.at[0],
                        recv_sem=z_recv.at[core],
                        device_id=(t, z, o),
                        device_id_type=MESH,
                    ).wait_recv()

        spread(jnp.where(c == 0, half - STEP * k, STEP * k + 2))
        row = jnp.where(c == 0, half - STEP * k, STEP * k)
        lhs = jnp.concatenate(
            [xs[:, pl.ds(row + a, STEP)].reshape(frames * flat, 3 * cin) for a in range(3)],
            axis=1,
        )
        drive = jnp.dot(lhs, w1[...], preferred_element_type=jnp.float32)
        running = drive[0:flat]
        local[k, 0] = running
        for f in range(1, frames):
            running = decay[f : f + 1, :] * running + drive[f * flat : (f + 1) * flat]
            local[k, f] = running

    def carry_copy(k):
        return pltpu.make_async_remote_copy(
            src_ref=carry_out.at[k],
            dst_ref=carry_in.at[k],
            send_sem=carry_send.at[k],
            recv_sem=carry_recv.at[k],
            device_id=(t + 1, z, c),
            device_id_type=MESH,
        )

    def out_copies(k):
        row = jnp.where(c == 0, half - STEP * k, STEP * k - 2)
        to = out_ref.at[:, pl.ds(half * c + row, STEP)]
        own = pltpu.make_async_copy(
            result.at[:, pl.ds(row, STEP), own_cols], to, out_sem.at[k]
        )
        far = pltpu.make_async_remote_copy(
            src_ref=result.at[:, pl.ds(row, STEP), other_cols],
            dst_ref=to,
            send_sem=out_send.at[k],
            recv_sem=out_recv.at[k],
            device_id=(t, z, o),
            device_id_type=MESH,
        )
        return own, far

    def mix_chunk(k):
        row = jnp.where(c == 0, half - STEP * k, STEP * k - 2)
        lhs = jnp.concatenate(
            [st[:, pl.ds(row + a, STEP)].reshape(frames * flat, state) for a in range(3)],
            axis=1,
        )
        taps = jnp.dot(lhs, w2[...], preferred_element_type=jnp.float32)
        at = columns(frames * flat)
        left = jnp.where(at == 0, 0.0, pltpu.roll(taps[:, 0:cin], 1, 0))
        right = jnp.where(
            at == width - 1, 0.0, pltpu.roll(taps[:, 2 * cin : 3 * cin], frames * flat - 1, 0)
        )
        latent = xp[:, pl.ds(row + 2, STEP)].reshape(frames * flat, cin).astype(jnp.float32)
        mixed = left + taps[:, cin : 2 * cin] + right + skip[...] * latent
        result[:, pl.ds(row, STEP)] = mixed.astype(result.dtype).reshape(
            frames, STEP, width, cin
        )
        for copy in out_copies(k):
            copy.start()

    def forward_chunk(k):
        @pl.when(t > 0)
        def _():
            carry_copy(k).wait_recv()

        @pl.when(has_next)
        def _():
            factor = decay[0:1, :]
            for f in range(1, frames):
                factor = factor * decay[f : f + 1, :]
            ahead = factor * carry_in[k].astype(jnp.float32) + local[k, frames - 1]
            carry_out[k] = ahead.astype(carry_out.dtype)
            carry_copy(k).start()

    def finish_chunk(k):
        row = jnp.where(c == 0, half - STEP * k, STEP * k)
        incoming = carry_in[k].astype(jnp.float32)
        product = decay[0:1, :]
        for f in range(frames):
            if f:
                product = product * decay[f : f + 1, :]
            now = (local[k, f] + product * incoming).astype(st.dtype)
            st[f, pl.ds(row, STEP)] = now.reshape(STEP, width, state)

        @pl.when(k == chunks - 1)
        def _():
            @pl.when(jnp.logical_and(c == 0, z == 0))
            def _():
                st[:, 0:1] = jnp.zeros((frames, 1, width, state), st.dtype)

            @pl.when(jnp.logical_and(c == 1, z == tiles - 1))
            def _():
                st[:, half + 1 : half + 2] = jnp.zeros((frames, 1, width, state), st.dtype)

        @pl.when(k > 0)
        def _():
            mix_chunk(k)

    lag = jnp.minimum(LAG * t, chunks)
    for copy in w2_loads:
        copy.wait()

    def turn(j, carried):
        @pl.when(j < chunks)
        def _():
            drive_chunk(j)

        @pl.when(jnp.logical_and(j >= lag, j - lag < chunks))
        def _():
            forward_chunk(j - lag)

        @pl.when(j >= chunks)
        def _():
            finish_chunk(j - chunks)

        return carried

    lax.fori_loop(0, 2 * chunks, turn, 0)

    side.wait_send()

    @pl.when(has_down)
    def _():
        to_down().wait_send()

    @pl.when(has_up)
    def _():
        to_up().wait_send()

    def finish(k, carried):
        @pl.when(has_next)
        def _():
            carry_copy(k).wait_send()

        @pl.when(k > 0)
        def _():
            own, far = out_copies(k)
            own.wait()
            far.wait_send()
            row = jnp.where(o == 0, half - STEP * k, STEP * k - 2)
            pltpu.make_async_remote_copy(
                src_ref=result.at[:, pl.ds(0, STEP), own_cols],
                dst_ref=out_ref.at[:, pl.ds(half * o + row, STEP)],
                send_sem=out_send.at[k],
                recv_sem=out_recv.at[k],
                device_id=(t, z, o),
                device_id_type=MESH,
            ).wait_recv()

        return carried

    lax.fori_loop(0, chunks, finish, 0)


def on_device(latent_video, input_kernel, output_kernel, decay_rate, skip_gain):
    frames, tile_h, tile_w, cin = latent_video.shape
    state = input_kernel.shape[3]
    blocks = lax.axis_size("tm")
    tiles = lax.axis_size("rows")
    half = tile_h // 2
    width = 2 * tile_w
    chunks = (half + 2) // STEP
    flat = STEP * width
    dma = pltpu.SemaphoreType.DMA
    bf16, f32 = jnp.bfloat16, jnp.float32
    pixels = frames * tile_h * tile_w
    return pl.pallas_call(
        functools.partial(layer_kernel, blocks, tiles),
        out_shape=jax.ShapeDtypeStruct(latent_video.shape, bf16),
        in_specs=[pl.BlockSpec(memory_space=pl.ANY)] * 5,
        out_specs=pl.BlockSpec(memory_space=pl.ANY),
        scratch_shapes=[
            pltpu.VMEM((frames, half + 4, width, cin), bf16),
            pltpu.VMEM((frames, half + 4, width, 3 * cin), bf16),
            pltpu.VMEM((chunks, frames, flat, state), f32),
            pltpu.VMEM((frames, half + 2, width, state), bf16),
            pltpu.VMEM((9 * cin, state), bf16),
            pltpu.VMEM((3 * state, 3 * cin), bf16),
            pltpu.VMEM((frames, state), f32),
            pltpu.VMEM((1, cin), f32),
            pltpu.VMEM((chunks, flat, state), bf16),
            pltpu.VMEM((chunks, flat, state), bf16),
            pltpu.VMEM((frames, half, width, cin), bf16),
            dma((4,)),
            dma((9,)),
            dma,
            dma,
            dma((2,)),
            dma((2,)),
            dma((chunks,)),
            dma((chunks,)),
            dma((chunks,)),
            dma((chunks,)),
            dma((chunks,)),
        ],
        compiler_params=pltpu.CompilerParams(
            collective_id=0, has_side_effects=True, vmem_limit_bytes=64 * 1024 * 1024
        ),
        cost_estimate=pl.CostEstimate(
            flops=4 * pixels * 9 * cin * state, bytes_accessed=8 * pixels * cin, transcendentals=0
        ),
    )(
        latent_video,
        input_kernel.reshape(9 * cin, state),
        output_kernel,
        decay_rate,
        skip_gain.reshape(1, cin),
    )


def solution(mesh):
    return jax.shard_map(
        on_device,
        mesh=mesh,
        in_specs=(P("tm", "rows", "cols", None), P(), P(), P("tm", None), P()),
        out_specs=P("tm", "rows", "cols", None),
        check_vma=False,
    )
```

```python
import functools

import jax
import jax.numpy as jnp
from jax import lax
from jax.experimental import pallas as pl
from jax.experimental.pallas import tpu as pltpu
from jax.sharding import PartitionSpec as P

MESH = pl.DeviceIdType.MESH
STEP = 2
LAG = 3


def layer_kernel(
    blocks, tiles, x_ref, w1_ref, w2_ref, decay_ref, skip_ref, out_ref,
    xp, xs, local, st, w1, w2, decay, skip, carry_in, pair_in, pair_decay, own_decay, carry_out, result,
    load_sem, w2_sem, side_send, side_recv, z_send, z_recv,
    decay_send, decay_recv, carry_send, far_send, carry_recv, pair_recv, out_sem, out_send, out_recv,
):
    frames, tile_h, tile_w, cin = x_ref.shape
    state = w1.shape[1]
    half = tile_h // 2
    width = 2 * tile_w
    chunks = (half + 2) // STEP
    flat = STEP * width
    t = lax.axis_index("tm")
    z = lax.axis_index("rows")
    c = lax.axis_index("cols")
    o = 1 - c
    has_up = z > 0
    has_down = z < tiles - 1
    odd = lax.rem(t, 2) == 1
    even = lax.rem(t, 2) == 0
    has_next = t < blocks - 1
    has_far = jnp.logical_and(odd, t < blocks - 2)
    has_carry = t > 1
    own_cols = pl.ds(pl.multiple_of(c * tile_w, tile_w), tile_w)
    other_cols = pl.ds(pl.multiple_of(o * tile_w, tile_w), tile_w)

    loads = [
        pltpu.make_async_copy(
            x_ref.at[:, pl.ds((half - 2) * c, half + 2)],
            xp.at[:, pl.ds(2 * o, half + 2), own_cols],
            load_sem.at[0],
        ),
        pltpu.make_async_copy(w1_ref, w1, load_sem.at[1]),
        pltpu.make_async_copy(decay_ref, decay, load_sem.at[2]),
        pltpu.make_async_copy(skip_ref, skip, load_sem.at[3]),
    ]
    w2_loads = [
        pltpu.make_async_copy(
            w2_ref.at[a, b],
            w2.at[pl.ds(a * state, state), pl.ds(b * cin, cin)],
            w2_sem.at[3 * a + b],
        )
        for a in range(3)
        for b in range(3)
    ]
    for copy in loads + w2_loads:
        copy.start()

    barrier = pltpu.get_barrier_semaphore()
    up_side = jnp.logical_and(c == 0, has_up)
    down_side = jnp.logical_and(c == 1, has_down)
    pl.semaphore_signal(barrier, inc=1, device_id=(t, z, o), device_id_type=MESH)

    @pl.when(up_side)
    def _():
        for core in range(2):
            pl.semaphore_signal(barrier, inc=1, device_id=(t, z - 1, core), device_id_type=MESH)

    @pl.when(down_side)
    def _():
        for core in range(2):
            pl.semaphore_signal(barrier, inc=1, device_id=(t, z + 1, core), device_id_type=MESH)

    @pl.when(t > 0)
    def _():
        pl.semaphore_signal(barrier, inc=1, device_id=(t - 1, z, c), device_id_type=MESH)

    @pl.when(jnp.logical_and(odd, has_carry))
    def _():
        pl.semaphore_signal(barrier, inc=1, device_id=(t - 2, z, c), device_id_type=MESH)

    @pl.when(jnp.logical_and(c == 0, z == 0))
    def _():
        xp[:, 0:2] = jnp.zeros((frames, 2, width, cin), xp.dtype)

    @pl.when(jnp.logical_and(c == 1, z == tiles - 1))
    def _():
        xp[:, half + 2 : half + 4] = jnp.zeros((frames, 2, width, cin), xp.dtype)

    @pl.when(t < 2)
    def _():
        carry_in[...] = jnp.zeros_like(carry_in)

    @pl.when(even)
    def _():
        pair_in[...] = jnp.zeros_like(pair_in)
        pair_decay[...] = jnp.ones_like(pair_decay)

    expected = (
        1
        + has_up.astype(jnp.int32)
        + has_down.astype(jnp.int32)
        + has_next.astype(jnp.int32)
        + has_far.astype(jnp.int32)
    )
    pl.semaphore_wait(barrier, expected)

    side = pltpu.make_async_remote_copy(
        src_ref=x_ref.at[:, pl.ds((half - 2) * o, half + 2)],
        dst_ref=xp.at[:, pl.ds(2 * c, half + 2), own_cols],
        send_sem=side_send,
        recv_sem=side_recv,
        device_id=(t, z, o),
        device_id_type=MESH,
    )
    side.start()

    def to_down():
        return pltpu.make_async_remote_copy(
            src_ref=x_ref.at[:, pl.ds(tile_h - 2, 2)],
            dst_ref=xp.at[:, pl.ds(0, 2), own_cols],
            send_sem=z_send.at[0],
            recv_sem=z_recv.at[c],
            device_id=(t, z + 1, 0),
            device_id_type=MESH,
        )

    def to_up():
        return pltpu.make_async_remote_copy(
            src_ref=x_ref.at[:, pl.ds(0, 2)],
            dst_ref=xp.at[:, pl.ds(half + 2, 2), own_cols],
            send_sem=z_send.at[1],
            recv_sem=z_recv.at[c],
            device_id=(t, z - 1, 1),
            device_id_type=MESH,
        )

    @pl.when(has_down)
    def _():
        to_down().start()

    @pl.when(has_up)
    def _():
        to_up().start()

    for copy in loads:
        copy.wait()

    block_decay = decay[0:1, :]
    for f in range(1, frames):
        block_decay = block_decay * decay[f : f + 1, :]
    own_decay[...] = jnp.broadcast_to(block_decay, own_decay.shape)

    def decay_copy():
        return pltpu.make_async_remote_copy(
            src_ref=own_decay,
            dst_ref=pair_decay,
            send_sem=decay_send,
            recv_sem=decay_recv,
            device_id=(t + 1, z, c),
            device_id_type=MESH,
        )

    sends_pair = jnp.logical_and(even, has_next)

    @pl.when(sends_pair)
    def _():
        decay_copy().start()

    pltpu.make_async_remote_copy(
        src_ref=x_ref.at[:, pl.ds((half - 2) * o, half + 2)],
        dst_ref=xp.at[:, pl.ds(2 * o, half + 2), other_cols],
        send_sem=side_send,
        recv_sem=side_recv,
        device_id=(t, z, o),
        device_id_type=MESH,
    ).wait_recv()

    def columns(rows):
        return lax.rem(lax.broadcasted_iota(jnp.int32, (rows, 128), 0), width)

    def spread(row):
        view = xp[:, pl.ds(row, STEP)].reshape(frames * flat, cin)
        wide = view.astype(jnp.float32)
        at = columns(frames * flat)
        left = jnp.where(at == 0, 0.0, pltpu.roll(wide, 1, 0))
        right = jnp.where(at == width - 1, 0.0, pltpu.roll(wide, frames * flat - 1, 0))
        shape = (frames, STEP, width, cin)
        xs[:, pl.ds(row, STEP), :, 0:cin] = left.astype(xs.dtype).reshape(shape)
        xs[:, pl.ds(row, STEP), :, cin : 2 * cin] = view.reshape(shape)
        xs[:, pl.ds(row, STEP), :, 2 * cin : 3 * cin] = right.astype(xs.dtype).reshape(shape)

    def drive_chunk(k):
        @pl.when(k == 0)
        def _():
            spread((half + 2) * o)

        @pl.when(k == chunks - 1)
        def _():
            @pl.when(jnp.logical_or(up_side, down_side))
            def _():
                for core in range(2):
                    rows = pl.ds((half + 2) * c, 2)
                    pltpu.make_async_remote_copy(
                        src_ref=x_ref.at[:, pl.ds(0, 2)],
                        dst_ref=xp.at[:, rows, pl.ds(core * tile_w, tile_w)],
                        send_sem=z_send.at[0],
                        recv_sem=z_recv.at[core],
                        device_id=(t, z, o),
                        device_id_type=MESH,
                    ).wait_recv()

        spread(jnp.where(c == 0, half - STEP * k, STEP * k + 2))
        row = jnp.where(c == 0, half - STEP * k, STEP * k)
        lhs = jnp.concatenate(
            [xs[:, pl.ds(row + a, STEP)].reshape(frames * flat, 3 * cin) for a in range(3)],
            axis=1,
        )
        drive = jnp.dot(lhs, w1[...], preferred_element_type=jnp.float32)
        running = drive[0:flat]
        local[k, 0] = running
        for f in range(1, frames):
            running = decay[f : f + 1, :] * running + drive[f * flat : (f + 1) * flat]
            local[k, f] = running

    def tm_copy(k, landing, send, recv, hop):
        return pltpu.make_async_remote_copy(
            src_ref=carry_out.at[k],
            dst_ref=landing.at[k],
            send_sem=send.at[k],
            recv_sem=recv.at[k],
            device_id=(t + hop, z, c),
            device_id_type=MESH,
        )

    def pair_copy(k):
        return tm_copy(k, pair_in, carry_send, pair_recv, 1)

    def next_copy(k):
        return tm_copy(k, carry_in, carry_send, carry_recv, 1)

    def far_copy(k):
        return tm_copy(k, carry_in, far_send, carry_recv, 2)

    def out_copies(k):
        row = jnp.where(c == 0, half - STEP * k, STEP * k - 2)
        to = out_ref.at[:, pl.ds(half * c + row, STEP)]
        own = pltpu.make_async_copy(
            result.at[:, pl.ds(row, STEP), own_cols], to, out_sem.at[k]
        )
        far = pltpu.make_async_remote_copy(
            src_ref=result.at[:, pl.ds(row, STEP), other_cols],
            dst_ref=to,
            send_sem=out_send.at[k],
            recv_sem=out_recv.at[k],
            device_id=(t, z, o),
            device_id_type=MESH,
        )
        return own, far

    def mix_chunk(k):
        row = jnp.where(c == 0, half - STEP * k, STEP * k - 2)
        lhs = jnp.concatenate(
            [st[:, pl.ds(row + a, STEP)].reshape(frames * flat, state) for a in range(3)],
            axis=1,
        )
        taps = jnp.dot(lhs, w2[...], preferred_element_type=jnp.float32)
        at = columns(frames * flat)
        left = jnp.where(at == 0, 0.0, pltpu.roll(taps[:, 0:cin], 1, 0))
        right = jnp.where(
            at == width - 1, 0.0, pltpu.roll(taps[:, 2 * cin : 3 * cin], frames * flat - 1, 0)
        )
        latent = xp[:, pl.ds(row + 2, STEP)].reshape(frames * flat, cin).astype(jnp.float32)
        mixed = left + taps[:, cin : 2 * cin] + right + skip[...] * latent
        result[:, pl.ds(row, STEP)] = mixed.astype(result.dtype).reshape(
            frames, STEP, width, cin
        )
        for copy in out_copies(k):
            copy.start()

    def incoming_of(k):
        return pair_in[k].astype(jnp.float32) + pair_decay[0:1, :] * carry_in[k].astype(jnp.float32)

    def pair_chunk(k):
        carry_out[k] = local[k, frames - 1].astype(carry_out.dtype)
        pair_copy(k).start()

    def forward_chunk(k):
        @pl.when(k == 0)
        def _():
            decay_copy().wait_recv()

        pair_copy(k).wait_recv()

        @pl.when(has_carry)
        def _():
            next_copy(k).wait_recv()

        @pl.when(has_next)
        def _():
            ahead = own_decay[0:1, :] * incoming_of(k) + local[k, frames - 1]
            carry_out[k] = ahead.astype(carry_out.dtype)
            next_copy(k).start()

            @pl.when(has_far)
            def _():
                far_copy(k).start()

    def finish_chunk(k):
        row = jnp.where(c == 0, half - STEP * k, STEP * k)
        incoming = incoming_of(k)
        product = decay[0:1, :]
        for f in range(frames):
            if f:
                product = product * decay[f : f + 1, :]
            now = (local[k, f] + product * incoming).astype(st.dtype)
            st[f, pl.ds(row, STEP)] = now.reshape(STEP, width, state)

        @pl.when(k == chunks - 1)
        def _():
            @pl.when(jnp.logical_and(c == 0, z == 0))
            def _():
                st[:, 0:1] = jnp.zeros((frames, 1, width, state), st.dtype)

            @pl.when(jnp.logical_and(c == 1, z == tiles - 1))
            def _():
                st[:, half + 1 : half + 2] = jnp.zeros((frames, 1, width, state), st.dtype)

        @pl.when(k > 0)
        def _():
            mix_chunk(k)

    for copy in w2_loads:
        copy.wait()

    def turn(j, carried):
        @pl.when(j < chunks)
        def _():
            drive_chunk(j)

            @pl.when(sends_pair)
            def _():
                pair_chunk(j)

        since = j - LAG
        paced = (2 * since + 1) // 3

        @pl.when((t == 1) & (since >= 0) & (lax.rem(since + 3, 3) != 1) & (paced < chunks))
        def _():
            forward_chunk(paced)

        @pl.when(j >= chunks)
        def _():
            @pl.when(odd & has_carry)
            def _():
                forward_chunk(j - chunks)

            @pl.when(even & has_carry)
            def _():
                next_copy(j - chunks).wait_recv()

            finish_chunk(j - chunks)

        return carried

    lax.fori_loop(0, 2 * chunks, turn, 0)

    side.wait_send()

    @pl.when(sends_pair)
    def _():
        decay_copy().wait_send()

    @pl.when(has_down)
    def _():
        to_down().wait_send()

    @pl.when(has_up)
    def _():
        to_up().wait_send()

    def finish(k, carried):
        @pl.when(has_next)
        def _():
            next_copy(k).wait_send()

        @pl.when(has_far)
        def _():
            far_copy(k).wait_send()

        @pl.when(k > 0)
        def _():
            own, far = out_copies(k)
            own.wait()
            far.wait_send()
            row = jnp.where(o == 0, half - STEP * k, STEP * k - 2)
            pltpu.make_async_remote_copy(
                src_ref=result.at[:, pl.ds(0, STEP), own_cols],
                dst_ref=out_ref.at[:, pl.ds(half * o + row, STEP)],
                send_sem=out_send.at[k],
                recv_sem=out_recv.at[k],
                device_id=(t, z, o),
                device_id_type=MESH,
            ).wait_recv()

        return carried

    lax.fori_loop(0, chunks, finish, 0)


def on_device(latent_video, input_kernel, output_kernel, decay_rate, skip_gain):
    frames, tile_h, tile_w, cin = latent_video.shape
    state = input_kernel.shape[3]
    blocks = lax.axis_size("tm")
    tiles = lax.axis_size("rows")
    half = tile_h // 2
    width = 2 * tile_w
    chunks = (half + 2) // STEP
    flat = STEP * width
    dma = pltpu.SemaphoreType.DMA
    bf16, f32 = jnp.bfloat16, jnp.float32
    pixels = frames * tile_h * tile_w
    return pl.pallas_call(
        functools.partial(layer_kernel, blocks, tiles),
        out_shape=pltpu.VMEM(latent_video.shape, bf16),
        in_specs=[pl.BlockSpec(memory_space=pl.ANY)] * 5,
        out_specs=pl.BlockSpec(memory_space=pltpu.VMEM),
        scratch_shapes=[
            pltpu.VMEM((frames, half + 4, width, cin), bf16),
            pltpu.VMEM((frames, half + 4, width, 3 * cin), bf16),
            pltpu.VMEM((chunks, frames, flat, state), f32),
            pltpu.VMEM((frames, half + 2, width, state), bf16),
            pltpu.VMEM((9 * cin, state), bf16),
            pltpu.VMEM((3 * state, 3 * cin), bf16),
            pltpu.VMEM((frames, state), f32),
            pltpu.VMEM((1, cin), f32),
            pltpu.VMEM((chunks, flat, state), bf16),
            pltpu.VMEM((chunks, flat, state), bf16),
            pltpu.VMEM((8, state), f32),
            pltpu.VMEM((8, state), f32),
            pltpu.VMEM((chunks, flat, state), bf16),
            pltpu.VMEM((frames, half, width, cin), bf16),
            dma((4,)),
            dma((9,)),
            dma,
            dma,
            dma((2,)),
            dma((2,)),
            dma,
            dma,
            dma((chunks,)),
            dma((chunks,)),
            dma((chunks,)),
            dma((chunks,)),
            dma((chunks,)),
            dma((chunks,)),
            dma((chunks,)),
        ],
        compiler_params=pltpu.CompilerParams(
            collective_id=0, has_side_effects=True, vmem_limit_bytes=62 * 1024 * 1024
        ),
        cost_estimate=pl.CostEstimate(
            flops=4 * pixels * 9 * cin * state, bytes_accessed=8 * pixels * cin, transcendentals=0
        ),
    )(
        latent_video,
        input_kernel.reshape(9 * cin, state),
        output_kernel,
        decay_rate,
        skip_gain.reshape(1, cin),
    )


def solution(mesh):
    return jax.shard_map(
        on_device,
        mesh=mesh,
        in_specs=(P("tm", "rows", "cols", None), P(), P(), P("tm", None), P()),
        out_specs=P("tm", "rows", "cols", None),
        check_vma=False,
    )
```

```python
import functools

import jax
import jax.numpy as jnp
from jax import lax
from jax.experimental import pallas as pl
from jax.experimental.pallas import tpu as pltpu
from jax.sharding import PartitionSpec as P

MESH = pl.DeviceIdType.MESH
STEP = 2
LAG = 2


def layer_kernel(
    blocks, tiles, x_ref, w1_ref, w2_ref, decay_ref, skip_ref, out_ref,
    xp, xs, local, st, w1, w2, decay, skip, carry_in, pair_in, pair_decay, own_decay, carry_out, result,
    load_sem, w2_sem, side_send, side_recv, z_send, z_recv,
    decay_send, decay_recv, carry_send, far_send, carry_recv, pair_recv, out_sem, out_send, out_recv,
):
    frames, tile_h, tile_w, cin = x_ref.shape
    state = w1.shape[1]
    half = tile_h // 2
    width = 2 * tile_w
    chunks = (half + 2) // STEP
    flat = STEP * width
    t = lax.axis_index("tm")
    z = lax.axis_index("rows")
    c = lax.axis_index("cols")
    o = 1 - c
    has_up = z > 0
    has_down = z < tiles - 1
    odd = lax.rem(t, 2) == 1
    even = lax.rem(t, 2) == 0
    has_next = t < blocks - 1
    has_far = jnp.logical_and(odd, t < blocks - 2)
    has_carry = t > 1
    own_cols = pl.ds(pl.multiple_of(c * tile_w, tile_w), tile_w)
    other_cols = pl.ds(pl.multiple_of(o * tile_w, tile_w), tile_w)

    loads = [
        pltpu.make_async_copy(
            x_ref.at[:, pl.ds((half - 2) * c, half + 2)],
            xp.at[:, pl.ds(2 * o, half + 2), own_cols],
            load_sem.at[0],
        ),
        pltpu.make_async_copy(w1_ref, w1, load_sem.at[1]),
        pltpu.make_async_copy(decay_ref, decay, load_sem.at[2]),
        pltpu.make_async_copy(skip_ref, skip, load_sem.at[3]),
    ]
    w2_loads = [
        pltpu.make_async_copy(
            w2_ref.at[a, b],
            w2.at[pl.ds(a * state, state), pl.ds(b * cin, cin)],
            w2_sem.at[3 * a + b],
        )
        for a in range(3)
        for b in range(3)
    ]
    for copy in loads + w2_loads:
        copy.start()

    barrier = pltpu.get_barrier_semaphore()
    up_side = jnp.logical_and(c == 0, has_up)
    down_side = jnp.logical_and(c == 1, has_down)
    pl.semaphore_signal(barrier, inc=1, device_id=(t, z, o), device_id_type=MESH)

    @pl.when(up_side)
    def _():
        for core in range(2):
            pl.semaphore_signal(barrier, inc=1, device_id=(t, z - 1, core), device_id_type=MESH)

    @pl.when(down_side)
    def _():
        for core in range(2):
            pl.semaphore_signal(barrier, inc=1, device_id=(t, z + 1, core), device_id_type=MESH)

    @pl.when(t > 0)
    def _():
        pl.semaphore_signal(barrier, inc=1, device_id=(t - 1, z, c), device_id_type=MESH)

    @pl.when(jnp.logical_and(odd, has_carry))
    def _():
        pl.semaphore_signal(barrier, inc=1, device_id=(t - 2, z, c), device_id_type=MESH)

    @pl.when(jnp.logical_and(c == 0, z == 0))
    def _():
        xp[:, 0:2] = jnp.zeros((frames, 2, width, cin), xp.dtype)

    @pl.when(jnp.logical_and(c == 1, z == tiles - 1))
    def _():
        xp[:, half + 2 : half + 4] = jnp.zeros((frames, 2, width, cin), xp.dtype)

    @pl.when(t < 2)
    def _():
        carry_in[...] = jnp.zeros_like(carry_in)

    @pl.when(even)
    def _():
        pair_in[...] = jnp.zeros_like(pair_in)
        pair_decay[...] = jnp.ones_like(pair_decay)

    expected = (
        1
        + has_up.astype(jnp.int32)
        + has_down.astype(jnp.int32)
        + has_next.astype(jnp.int32)
        + has_far.astype(jnp.int32)
    )
    pl.semaphore_wait(barrier, expected)

    def side_copy(k, rows, core, columns_at):
        start = half * (1 - core) if rows == 2 * STEP else jnp.where(
            core == 0, half - STEP * k, STEP * k + 2
        )
        sent = start - 2 + half * core
        return pltpu.make_async_remote_copy(
            src_ref=x_ref.at[:, pl.ds(sent, rows)],
            dst_ref=xp.at[:, pl.ds(start, rows), columns_at],
            send_sem=side_send.at[k],
            recv_sem=side_recv.at[k],
            device_id=(t, z, o),
            device_id_type=MESH,
        )

    sides = [
        side_copy(k, 2 * STEP if k == 0 else STEP, o, own_cols) for k in range(chunks - 1)
    ]
    for copy in sides:
        copy.start()

    def to_down():
        return pltpu.make_async_remote_copy(
            src_ref=x_ref.at[:, pl.ds(tile_h - 2, 2)],
            dst_ref=xp.at[:, pl.ds(0, 2), own_cols],
            send_sem=z_send.at[0],
            recv_sem=z_recv.at[c],
            device_id=(t, z + 1, 0),
            device_id_type=MESH,
        )

    def to_up():
        return pltpu.make_async_remote_copy(
            src_ref=x_ref.at[:, pl.ds(0, 2)],
            dst_ref=xp.at[:, pl.ds(half + 2, 2), own_cols],
            send_sem=z_send.at[1],
            recv_sem=z_recv.at[c],
            device_id=(t, z - 1, 1),
            device_id_type=MESH,
        )

    @pl.when(has_down)
    def _():
        to_down().start()

    @pl.when(has_up)
    def _():
        to_up().start()

    for copy in loads:
        copy.wait()

    block_decay = decay[0:1, :]
    for f in range(1, frames):
        block_decay = block_decay * decay[f : f + 1, :]
    own_decay[...] = jnp.broadcast_to(block_decay, own_decay.shape)

    def decay_copy():
        return pltpu.make_async_remote_copy(
            src_ref=own_decay,
            dst_ref=pair_decay,
            send_sem=decay_send,
            recv_sem=decay_recv,
            device_id=(t + 1, z, c),
            device_id_type=MESH,
        )

    sends_pair = jnp.logical_and(even, has_next)

    @pl.when(sends_pair)
    def _():
        decay_copy().start()

    def columns(rows):
        return lax.rem(lax.broadcasted_iota(jnp.int32, (rows, 128), 0), width)

    def spread(row):
        view = xp[:, pl.ds(row, STEP)].reshape(frames * flat, cin)
        wide = view.astype(jnp.float32)
        at = columns(frames * flat)
        left = jnp.where(at == 0, 0.0, pltpu.roll(wide, 1, 0))
        right = jnp.where(at == width - 1, 0.0, pltpu.roll(wide, frames * flat - 1, 0))
        shape = (frames, STEP, width, cin)
        xs[:, pl.ds(row, STEP), :, 0:cin] = left.astype(xs.dtype).reshape(shape)
        xs[:, pl.ds(row, STEP), :, cin : 2 * cin] = view.reshape(shape)
        xs[:, pl.ds(row, STEP), :, 2 * cin : 3 * cin] = right.astype(xs.dtype).reshape(shape)

    def drive_chunk(k):
        @pl.when(k == 0)
        def _():
            side_copy(k, 2 * STEP, c, other_cols).wait_recv()
            spread((half + 2) * o)

        @pl.when((k > 0) & (k < chunks - 1))
        def _():
            side_copy(k, STEP, c, other_cols).wait_recv()

        @pl.when(k == chunks - 1)
        def _():
            @pl.when(jnp.logical_or(up_side, down_side))
            def _():
                for core in range(2):
                    rows = pl.ds((half + 2) * c, 2)
                    pltpu.make_async_remote_copy(
                        src_ref=x_ref.at[:, pl.ds(0, 2)],
                        dst_ref=xp.at[:, rows, pl.ds(core * tile_w, tile_w)],
                        send_sem=z_send.at[0],
                        recv_sem=z_recv.at[core],
                        device_id=(t, z, o),
                        device_id_type=MESH,
                    ).wait_recv()

        spread(jnp.where(c == 0, half - STEP * k, STEP * k + 2))
        row = jnp.where(c == 0, half - STEP * k, STEP * k)
        lhs = jnp.concatenate(
            [xs[:, pl.ds(row + a, STEP)].reshape(frames * flat, 3 * cin) for a in range(3)],
            axis=1,
        )
        drive = jnp.dot(lhs, w1[...], preferred_element_type=jnp.float32)
        running = drive[0:flat]
        local[k, 0] = running
        for f in range(1, frames):
            running = decay[f : f + 1, :] * running + drive[f * flat : (f + 1) * flat]
            local[k, f] = running

    def tm_copy(k, landing, send, recv, hop):
        return pltpu.make_async_remote_copy(
            src_ref=carry_out.at[k],
            dst_ref=landing.at[k],
            send_sem=send.at[k],
            recv_sem=recv.at[k],
            device_id=(t + hop, z, c),
            device_id_type=MESH,
        )

    def pair_copy(k):
        return tm_copy(k, pair_in, carry_send, pair_recv, 1)

    def next_copy(k):
        return tm_copy(k, carry_in, carry_send, carry_recv, 1)

    def far_copy(k):
        return tm_copy(k, carry_in, far_send, carry_recv, 2)

    def out_copies(k):
        row = jnp.where(c == 0, half - STEP * k, STEP * k - 2)
        to = out_ref.at[:, pl.ds(half * c + row, STEP)]
        own = pltpu.make_async_copy(
            result.at[:, pl.ds(row, STEP), own_cols], to, out_sem.at[k]
        )
        far = pltpu.make_async_remote_copy(
            src_ref=result.at[:, pl.ds(row, STEP), other_cols],
            dst_ref=to,
            send_sem=out_send.at[k],
            recv_sem=out_recv.at[k],
            device_id=(t, z, o),
            device_id_type=MESH,
        )
        return own, far

    def mix_chunk(k):
        row = jnp.where(c == 0, half - STEP * k, STEP * k - 2)
        lhs = jnp.concatenate(
            [st[:, pl.ds(row + a, STEP)].reshape(frames * flat, state) for a in range(3)],
            axis=1,
        )
        taps = jnp.dot(lhs, w2[...], preferred_element_type=jnp.float32)
        at = columns(frames * flat)
        left = jnp.where(at == 0, 0.0, pltpu.roll(taps[:, 0:cin], 1, 0))
        right = jnp.where(
            at == width - 1, 0.0, pltpu.roll(taps[:, 2 * cin : 3 * cin], frames * flat - 1, 0)
        )
        latent = xp[:, pl.ds(row + 2, STEP)].reshape(frames * flat, cin).astype(jnp.float32)
        mixed = left + taps[:, cin : 2 * cin] + right + skip[...] * latent
        result[:, pl.ds(row, STEP)] = mixed.astype(result.dtype).reshape(
            frames, STEP, width, cin
        )
        for copy in out_copies(k):
            copy.start()

    def incoming_of(k):
        return pair_in[k].astype(jnp.float32) + pair_decay[0:1, :] * carry_in[k].astype(jnp.float32)

    def pair_chunk(k):
        carry_out[k] = local[k, frames - 1].astype(carry_out.dtype)
        pair_copy(k).start()

    def forward_chunk(k):
        @pl.when(k == 0)
        def _():
            decay_copy().wait_recv()

        pair_copy(k).wait_recv()

        @pl.when(has_carry)
        def _():
            next_copy(k).wait_recv()

        @pl.when(has_next)
        def _():
            ahead = own_decay[0:1, :] * incoming_of(k) + local[k, frames - 1]
            carry_out[k] = ahead.astype(carry_out.dtype)
            next_copy(k).start()

            @pl.when(has_far)
            def _():
                far_copy(k).start()

    def finish_chunk(k):
        row = jnp.where(c == 0, half - STEP * k, STEP * k)
        incoming = incoming_of(k)
        product = decay[0:1, :]
        for f in range(frames):
            if f:
                product = product * decay[f : f + 1, :]
            now = (local[k, f] + product * incoming).astype(st.dtype)
            st[f, pl.ds(row, STEP)] = now.reshape(STEP, width, state)

        @pl.when(k == chunks - 1)
        def _():
            @pl.when(jnp.logical_and(c == 0, z == 0))
            def _():
                st[:, 0:1] = jnp.zeros((frames, 1, width, state), st.dtype)

            @pl.when(jnp.logical_and(c == 1, z == tiles - 1))
            def _():
                st[:, half + 1 : half + 2] = jnp.zeros((frames, 1, width, state), st.dtype)

        @pl.when(k > 0)
        def _():
            mix_chunk(k)

    for copy in w2_loads:
        copy.wait()

    def turn(j, carried):
        @pl.when(j < chunks)
        def _():
            drive_chunk(j)

            @pl.when(sends_pair)
            def _():
                pair_chunk(j)

        since = j - LAG
        paced = (2 * since + 1) // 3

        @pl.when((t == 1) & (since >= 0) & (lax.rem(since + 3, 3) != 1) & (paced < chunks))
        def _():
            forward_chunk(paced)

        @pl.when(j >= chunks)
        def _():
            @pl.when(odd & has_carry)
            def _():
                forward_chunk(j - chunks)

            @pl.when(even & has_carry)
            def _():
                next_copy(j - chunks).wait_recv()

            finish_chunk(j - chunks)

        return carried

    lax.fori_loop(0, 2 * chunks, turn, 0)

    for copy in sides:
        copy.wait_send()

    @pl.when(sends_pair)
    def _():
        decay_copy().wait_send()

    @pl.when(has_down)
    def _():
        to_down().wait_send()

    @pl.when(has_up)
    def _():
        to_up().wait_send()

    def finish(k, carried):
        @pl.when(has_next)
        def _():
            next_copy(k).wait_send()

        @pl.when(has_far)
        def _():
            far_copy(k).wait_send()

        @pl.when(k > 0)
        def _():
            own, far = out_copies(k)
            own.wait()
            far.wait_send()
            row = jnp.where(o == 0, half - STEP * k, STEP * k - 2)
            pltpu.make_async_remote_copy(
                src_ref=result.at[:, pl.ds(0, STEP), own_cols],
                dst_ref=out_ref.at[:, pl.ds(half * o + row, STEP)],
                send_sem=out_send.at[k],
                recv_sem=out_recv.at[k],
                device_id=(t, z, o),
                device_id_type=MESH,
            ).wait_recv()

        return carried

    lax.fori_loop(0, chunks, finish, 0)


def on_device(latent_video, input_kernel, output_kernel, decay_rate, skip_gain):
    frames, tile_h, tile_w, cin = latent_video.shape
    state = input_kernel.shape[3]
    blocks = lax.axis_size("tm")
    tiles = lax.axis_size("rows")
    half = tile_h // 2
    width = 2 * tile_w
    chunks = (half + 2) // STEP
    flat = STEP * width
    dma = pltpu.SemaphoreType.DMA
    bf16, f32 = jnp.bfloat16, jnp.float32
    pixels = frames * tile_h * tile_w
    return pl.pallas_call(
        functools.partial(layer_kernel, blocks, tiles),
        out_shape=pltpu.VMEM(latent_video.shape, bf16),
        in_specs=[pl.BlockSpec(memory_space=pl.ANY)] * 5,
        out_specs=pl.BlockSpec(memory_space=pltpu.VMEM),
        scratch_shapes=[
            pltpu.VMEM((frames, half + 4, width, cin), bf16),
            pltpu.VMEM((frames, half + 4, width, 3 * cin), bf16),
            pltpu.VMEM((chunks, frames, flat, state), f32),
            pltpu.VMEM((frames, half + 2, width, state), bf16),
            pltpu.VMEM((9 * cin, state), bf16),
            pltpu.VMEM((3 * state, 3 * cin), bf16),
            pltpu.VMEM((frames, state), f32),
            pltpu.VMEM((1, cin), f32),
            pltpu.VMEM((chunks, flat, state), bf16),
            pltpu.VMEM((chunks, flat, state), bf16),
            pltpu.VMEM((8, state), f32),
            pltpu.VMEM((8, state), f32),
            pltpu.VMEM((chunks, flat, state), bf16),
            pltpu.VMEM((frames, half, width, cin), bf16),
            dma((4,)),
            dma((9,)),
            dma((chunks - 1,)),
            dma((chunks - 1,)),
            dma((2,)),
            dma((2,)),
            dma,
            dma,
            dma((chunks,)),
            dma((chunks,)),
            dma((chunks,)),
            dma((chunks,)),
            dma((chunks,)),
            dma((chunks,)),
            dma((chunks,)),
        ],
        compiler_params=pltpu.CompilerParams(
            collective_id=0, has_side_effects=True, vmem_limit_bytes=62 * 1024 * 1024
        ),
        cost_estimate=pl.CostEstimate(
            flops=4 * pixels * 9 * cin * state, bytes_accessed=8 * pixels * cin, transcendentals=0
        ),
    )(
        latent_video,
        input_kernel.reshape(9 * cin, state),
        output_kernel,
        decay_rate,
        skip_gain.reshape(1, cin),
    )


def solution(mesh):
    return jax.shard_map(
        on_device,
        mesh=mesh,
        in_specs=(P("tm", "rows", "cols", None), P(), P(), P("tm", None), P()),
        out_specs=P("tm", "rows", "cols", None),
        check_vma=False,
    )
```
